128 devices in a mesh: ref: 2 (over core), lines: 8 (over y, z_hi), cells: 8 (over z_lo, x).
Axes of the slice: x: 4, y: 4, z: 4 (z_hi: 2, z_lo: 2; z = z_hi * 2 + z_lo), core: 2. Of those that a mesh axis runs over, the one named last changes fastest.
Arguments:
- sens: bfloat16 [32768, 128, 128], P(('lines', 'cells')), may hold values from -0.125 to 0.125
- block_rows: int32 [32768], P(('lines', 'cells')), may hold values from 0 to 31
- block_cols: int32 [32768], P(('lines', 'cells')), may hold values from 0 to 2047, as said below
- neighbours: int32 [6, 262144], P(None, ('lines', 'cells')), may hold values from 0 to 262143, as said below
- observed: float32 [262144], P(('lines', 'cells')), may hold values from -6 to 6
- data_weight: float32 [262144], P(('lines', 'cells')), may hold values from 0.3 to 5.2
- smallness: float32 [262144], P(('lines', 'cells')), may hold values from 0.1 to 1
- model: float32 [524288], P(('ref', 'lines', 'cells')), parts along dimension 0, may hold values from -6 to 6
- reference_model: float32 [524288], P(('ref', 'lines', 'cells')), parts along dimension 0, may hold values from -6 to 6
Outputs:
- update: float32 [524288], P(('ref', 'lines', 'cells')), parts along dimension 0
- cg_residual: float32 [524288], P(('ref', 'lines', 'cells')), parts along dimension 0
The draws below stay inside these ranges and needn't reach their ends.
There are 2 independent parts, one for each index of `ref`. The reference program is written for one: setup_inputs(seed, part) draws one part's arguments, and reference() takes and returns one part's arrays. A program takes and returns all parts, laid end to end along the dimension named above; an argument that names none is the same for every part. Nothing has to cross between parts.
Inputs may be any that keep to these rules, and one draw needn't show every extreme that they name: `block_cols`: devices hold aligned runs of 512 blocks; cell block c is owned by device c // 32. The blocks of one device name at most 16 cell blocks of any one owner, and in every draw one owner gets exactly 16 from every device. `neighbours`: A cell's own index stands for a missing neighbour; the relation is symmetric, and every neighbour lies within 1024 cells of its cell, some exactly that far.
All inputs are finite; a program needn't handle non-finite values.
Results may differ from the reference program's by a relative error of at most 0.0131.
Values may be sent and summed in bfloat16 or wider, within the bound.
No kernel may reach another device: no remote copies, remote signals or barrier semaphores. Data moves between devices by JAX's collectives and lax.ppermute only.
A program may use at most 64 MiB of HBM per device.

```python
import math
import jax
import jax.numpy as jnp
from jax import lax

BLK = 128
CELL_DEV = 4096
RB_DEV = 32
NB_DEV = 512
CG_STEPS = 3
PART_DEVS = 64
MODEL_CELLS = 262144
DATA_ALL = 262144
BLOCKS_ALL = 32768
CAP = 16


def draw_block_cols(key, part):
    key = jax.random.fold_in(key, 11)
    key_star, key_rest = jax.random.split(key, 2)
    col_blocks = CELL_DEV // 128
    star = jax.random.randint(key_star, (), 0, PART_DEVS).astype(jnp.int32)

    def sender(sender_key):
        key_pool, key_mix, key_within = jax.random.split(sender_key, 3)
        pool = jax.random.permutation(key_pool, (PART_DEVS - 1) * CAP).astype(jnp.int32) // CAP
        others = pool + (pool >= star).astype(jnp.int32)
        owners = jnp.concatenate([jnp.full((CAP,), 1, jnp.int32) * star, others[:NB_DEV - CAP]])
        owners = jax.random.permutation(key_mix, owners)
        within = jax.random.randint(key_within, (NB_DEV,), 0, col_blocks).astype(jnp.int32)
        return owners * col_blocks + within
    keys = jax.random.split(key_rest, PART_DEVS)
    return jax.vmap(sender)(keys).reshape(-1).astype(jnp.int32)


def draw_neighbours(key, part):
    key = jax.random.fold_in(key, 5)
    present = jax.random.randint(key, (3, MODEL_CELLS), 0, 8) < 7
    index = jnp.arange(MODEL_CELLS, dtype=jnp.int32)
    strides = [1, 32, CELL_DEV // 4]
    ahead = []
    behind = []
    for which in range(3):
        stride = strides[which]
        forward_cell = index + stride
        has_forward = present[which] & (forward_cell < MODEL_CELLS)
        ahead.append(jnp.where(has_forward, forward_cell, index))
        back_cell = index - stride
        has_back = (back_cell >= 0) & jnp.take(present[which], jnp.maximum(back_cell, 0))
        behind.append(jnp.where(has_back, back_cell, index))
    return jnp.stack(ahead + behind).astype(jnp.int32)


def draw_data_weight(key, part):
    key = jax.random.fold_in(key, 7)
    device = (jnp.arange(DATA_ALL) // (RB_DEV * 128)).astype(jnp.float32)
    ramp = jnp.sqrt(1.0 + 2.0 * device / max(PART_DEVS - 1, 1))
    base = jnp.exp(jax.random.uniform(key, (DATA_ALL,), jnp.float32, jnp.log(0.5), jnp.log(2.0)))
    return (base * ramp).astype(jnp.float32)


def set_ends(drawn, stream_key, least, high):
    dims = drawn.shape
    index_at = [jax.random.randint(jax.random.fold_in(stream_key, axis), (), 0, dims[axis]) for axis in range(len(dims))]
    drawn = drawn.at[tuple(index_at)].set(least)
    longest = dims.index(max(dims))
    index_at[longest] = (index_at[longest] + 1) % dims[longest]
    return drawn.at[tuple(index_at)].set(high)


def block_scale(key, shape, pieces, low, high):
    gain, own = 1.0, jax.random.fold_in(key, 6)
    for position, parts in pieces:
        steps = jnp.exp(jax.random.uniform(jax.random.fold_in(own, position), (parts,), jnp.float32, low / len(pieces), high / len(pieces)))
        gain = gain * jnp.repeat(steps, shape[position] // parts).reshape([-1 if axis == position else 1 for axis in range(len(shape))])
    return gain


def scatter_about(stream_key, extent, width, reach, pieces=(), kind=jnp.bfloat16):
    values = jax.random.normal(stream_key, extent, jnp.float32) * width
    if len(pieces) > 0:
        values = block_scale(stream_key, extent, pieces, -0.22, 0.18) * values
    return jnp.clip(values, min=-reach, max=reach).astype(kind)


def setup_inputs(seed: int = 0, part: int = 0) -> dict:
    key_list = jax.random.split(jax.random.key(seed), 10)
    own_keys = jax.random.split(jax.random.fold_in(key_list[9], part), 10)
    sens = scatter_about(key_list[0], (BLOCKS_ALL, BLK, BLK), (128 * NB_DEV // RB_DEV) ** -0.5, 0.125, ((0, 64),))
    block_rows = set_ends(jax.random.randint(key_list[1], (BLOCKS_ALL,), 0, RB_DEV), jax.random.fold_in(key_list[1], 1), 0, RB_DEV - 1).astype(jnp.int32)
    block_cols = draw_block_cols(jax.random.fold_in(key_list[9], 71), part)
    neighbours = draw_neighbours(jax.random.fold_in(key_list[9], 71), part)
    observed = scatter_about(key_list[4], (DATA_ALL,), 1.0, 6.0, ((0, 64),), jnp.float32)
    data_weight = draw_data_weight(jax.random.fold_in(key_list[9], 71), part)
    smallness = jnp.clip(jnp.exp(math.log(1.0) - 2.3025851 * jax.random.uniform(key_list[6], (MODEL_CELLS,), jnp.float32) ** block_scale(key_list[6], (MODEL_CELLS,), ((0, 64),), -0.2, 0.2)), 0.1, 1.0)
    model = scatter_about(own_keys[7], (MODEL_CELLS,), 1.0, 6.0, ((0, 64),), jnp.float32)
    reference_model = scatter_about(own_keys[8], (MODEL_CELLS,), 1.0, 6.0, ((0, 64),), jnp.float32)
    return {"sens": sens, "block_rows": block_rows, "block_cols": block_cols, "neighbours": neighbours, "observed": observed, "data_weight": data_weight, "smallness": smallness, "model": model, "reference_model": reference_model}


beta_reg = 0.5


def round_half(values):
    return lax.optimization_barrier(values.astype(jnp.bfloat16)).astype(jnp.float32)


def forward_all(sens, row_global, block_cols, vector):
    blocks = round_half(vector).reshape(-1, 128)

    def visit(total, span):
        slab, rows_here, cols_here = span
        products = jnp.einsum("bij,bj->bi", slab.astype(jnp.float32), blocks[cols_here], precision=lax.Precision.HIGHEST)
        return total.at[rows_here].add(products), None

    start_total = jnp.zeros((DATA_ALL // 128, 128), jnp.float32)
    total, unused = lax.scan(visit, start_total, (sens.reshape(PART_DEVS, NB_DEV, 128, 128), row_global.reshape(PART_DEVS, NB_DEV), block_cols.reshape(PART_DEVS, NB_DEV)))
    return total.reshape(-1)


def backward_all(sens, row_global, block_cols, weighted):
    values = weighted.astype(jnp.float32).reshape(-1, 128)

    def visit(total, span):
        slab, rows_here, cols_here = span
        partial_terms = jnp.einsum("bij,bi->bj", slab.astype(jnp.float32), values[rows_here], precision=lax.Precision.HIGHEST)
        return total.at[cols_here].add(partial_terms), None

    start_total = jnp.zeros((MODEL_CELLS // 128, 128), jnp.float32)
    total, unused = lax.scan(visit, start_total, (sens.reshape(PART_DEVS, NB_DEV, 128, 128), row_global.reshape(PART_DEVS, NB_DEV), block_cols.reshape(PART_DEVS, NB_DEV)))
    return total.reshape(-1)


def smooth(vector, smallness, neighbours):
    return (smallness + 6.0) * vector - jnp.sum(vector[neighbours], axis=0)


def reference(sens, block_rows, block_cols, neighbours, observed, data_weight, smallness, model, reference_model):
    row_global = (jnp.arange(BLOCKS_ALL, dtype=jnp.int32) // NB_DEV) * RB_DEV + block_rows
    weight_sq = data_weight * data_weight
    misfit = (weight_sq * (forward_all(sens, row_global, block_cols, model) - observed)).astype(jnp.bfloat16)
    right_side = -(backward_all(sens, row_global, block_cols, misfit) + beta_reg * smooth(model - reference_model, smallness, neighbours))
    update = jnp.zeros_like(right_side)
    residual = right_side
    direction = right_side
    norm_now = jnp.sum(residual * residual)
    for iteration in range(CG_STEPS):
        predicted = forward_all(sens, row_global, block_cols, direction)
        weighted = (weight_sq * predicted).astype(jnp.bfloat16)
        bent = smooth(direction, smallness, neighbours)
        image = backward_all(sens, row_global, block_cols, weighted) + beta_reg * bent
        curvature = jnp.sum(predicted * weighted.astype(jnp.float32)) + beta_reg * jnp.sum(direction * bent)
        alpha = norm_now / curvature
        update = update + alpha * direction
        residual = residual - alpha * image
        norm_next = jnp.sum(residual * residual)
        direction = residual + (norm_next / norm_now) * direction
        norm_now = norm_next
    return update, residual
```

```python
import functools

import jax
import jax.numpy as jnp
from jax import lax
from jax.experimental import pallas as pl
from jax.experimental.pallas import tpu as pltpu
from jax.sharding import PartitionSpec as P

CG_STEPS = 3
beta_reg = 0.5

AXES = ("lines", "cells")
UNROLL = 4
GROUP_DEVS = 64
ROWS = 32
CELL_ROWS = 32
TABLE = GROUP_DEVS * CELL_ROWS
EXTRA = 16
F32 = jnp.float32
BF16 = jnp.bfloat16


def total(x):
    return jnp.sum(jnp.sum(x, axis=0, keepdims=True), axis=1, keepdims=True)


def smooth_from(win, nb_ref, small, offset):
    sub = lax.broadcasted_iota(jnp.int32, (8, 128), 0)
    pieces = []
    for g in range(CELL_ROWS // 8):
        acc = jnp.zeros((8, 128), F32)
        lanes = []
        deltas = []
        for k in range(6):
            index = nb_ref[k, pl.ds(8 * g, 8), :] - offset + 1024
            lanes.append(index & 127)
            deltas.append((index >> 7) - 8 * g - sub)
        for delta in range(17):
            source = win[pl.ds(8 * g + delta, 8), :]
            for k in range(6):
                picked = jnp.take_along_axis(source, lanes[k], axis=1, mode="promise_in_bounds")
                acc = acc + jnp.where(deltas[k] == delta, picked, 0.0)
        own = win[pl.ds(8 * g + 8, 8), :]
        pieces.append((small[pl.ds(8 * g, 8), :] + 6.0) * own - acc)
    return jnp.concatenate(pieces, axis=0)


def forward_rows(starts, order, cols, sens, tab, accs):
    def row(r, _):
        first = starts[r]
        count = (starts[r + 1] - first) // UNROLL

        def group(g, acc):
            for q in range(UNROLL):
                k = first + g * UNROLL + q
                acc = acc + sens[order[k]].astype(F32) * tab[pl.ds(cols[k], 1), :]
            return acc

        accs[r] = lax.fori_loop(0, count, group, jnp.zeros((128, 128), F32))
        return 0

    lax.fori_loop(0, ROWS, row, 0)


def reduce_rows(accs, pred):
    def rows(g, _):
        for q in range(4):
            r = g * 4 + q
            pred[pl.ds(r, 1), :] = jnp.sum(accs[r].T, axis=0, keepdims=True)
        return 0

    lax.fori_loop(0, ROWS // 4, rows, 0)


def backward_rows(starts, order, cols, sens, us, spread):
    spread[...] = jnp.zeros_like(spread)

    def row(r, _):
        first = starts[r]
        count = (starts[r + 1] - first) // UNROLL
        weights = jnp.broadcast_to(us[pl.ds(r, 1), :], (128, 128)).T

        def group(g, _):
            for q in range(UNROLL):
                k = first + g * UNROLL + q
                term = jnp.sum(sens[order[k]].astype(F32) * weights, axis=0, keepdims=True)
                spread[pl.ds(cols[k], 1), :] += term
            return 0

        lax.fori_loop(0, count, group, 0)
        return 0

    lax.fori_loop(0, ROWS, row, 0)


def write_payload(out, spread, scalar):
    if scalar is None:
        tail = jnp.zeros((EXTRA, 128), BF16)
    else:
        high = scalar.astype(BF16).astype(F32)
        middle = (scalar - high).astype(BF16).astype(F32)
        low = scalar - high - middle
        sub = lax.broadcasted_iota(jnp.int32, (EXTRA, 128), 0)
        lane = lax.broadcasted_iota(jnp.int32, (EXTRA, 128), 1)
        place = sub * 128 + lane
        tail = jnp.where(
            place == 0, high, jnp.where(place == 1, middle, jnp.where(place == 2, low, 0.0))
        ).astype(BF16)

    def owner(o, _):
        base = pl.multiple_of(o * CELL_ROWS, CELL_ROWS)
        out[o, pl.ds(0, CELL_ROWS), :] = spread[pl.ds(base, CELL_ROWS), :].astype(BF16)
        out[o, pl.ds(CELL_ROWS, EXTRA), :] = tail
        return 0

    lax.fori_loop(0, GROUP_DEVS, owner, 0)


def start_kernel(
    starts, order, cols, me, sens, recv, diff, observed, data_weight, nb, small,
    out, bent_out, tab, accs, pred, spread, win,
):
    def owner(o, _):
        base = pl.multiple_of(o * CELL_ROWS, CELL_ROWS)
        tab[pl.ds(base, CELL_ROWS), :] = recv[o, pl.ds(0, CELL_ROWS), :].astype(F32)
        return 0

    lax.fori_loop(0, GROUP_DEVS, owner, 0)
    tab[pl.ds(TABLE, 8), :] = jnp.zeros((8, 128), F32)
    mine = me[0]
    before = jnp.maximum(mine - 1, 0)
    after = jnp.minimum(mine + 1, GROUP_DEVS - 1)
    win[pl.ds(0, 8), :] = recv[before, pl.ds(CELL_ROWS, 16), :].astype(F32)[8:16]
    win[pl.ds(8, CELL_ROWS), :] = diff[...]
    win[pl.ds(8 + CELL_ROWS, 8), :] = recv[after, pl.ds(CELL_ROWS, 16), :].astype(F32)[0:8]
    bent_out[...] = smooth_from(win, nb, small, mine * (CELL_ROWS * 128))
    forward_rows(starts, order, cols, sens, tab, accs)
    reduce_rows(accs, pred)
    weight = data_weight[...]
    misfit = weight * weight * (pred[...] - observed[...])
    pred[...] = misfit.astype(BF16).astype(F32)
    backward_rows(starts, order, cols, sens, pred, spread)
    write_payload(out, spread, None)


def step_kernel(
    first_step,
    starts, order, cols, me, sens, recv, residual, direction, d_all_in, norm_in, data_weight, nb, small,
    out, bent_out, d_out, d_all_out, norm_out, tab, accs, pred, spread, win,
):
    def squares(o, acc):
        r = recv[o].astype(F32)
        return acc + r * r

    acc = lax.fori_loop(0, GROUP_DEVS, squares, jnp.zeros((CELL_ROWS, 128), F32))
    norm = total(acc)
    norm_out[...] = jnp.broadcast_to(norm, (8, 128))
    beta = None if first_step else norm / norm_in[0:1, 0:1]

    def owner(o, _):
        base = pl.multiple_of(o * CELL_ROWS, CELL_ROWS)
        d = recv[o].astype(F32)
        if not first_step:
            d = d + beta * d_all_in[pl.ds(base, CELL_ROWS), :]
        d_all_out[pl.ds(base, CELL_ROWS), :] = d
        tab[pl.ds(base, CELL_ROWS), :] = d.astype(BF16).astype(F32)
        return 0

    lax.fori_loop(0, GROUP_DEVS, owner, 0)
    tab[pl.ds(TABLE, 8), :] = jnp.zeros((8, 128), F32)
    d_own = residual[...]
    if not first_step:
        d_own = d_own + beta * direction[...]
    d_out[...] = d_own
    mine = me[0]
    base = mine * CELL_ROWS
    before = pl.multiple_of(jnp.maximum(base - 8, 0), 8)
    after = pl.multiple_of(jnp.minimum(base + CELL_ROWS, TABLE - 8), 8)
    win[pl.ds(0, 8), :] = d_all_out[pl.ds(before, 8), :]
    win[pl.ds(8, CELL_ROWS), :] = d_own
    win[pl.ds(8 + CELL_ROWS, 8), :] = d_all_out[pl.ds(after, 8), :]
    bent = smooth_from(win, nb, small, mine * (CELL_ROWS * 128))
    bent_out[...] = bent
    forward_rows(starts, order, cols, sens, tab, accs)
    reduce_rows(accs, pred)
    weight = data_weight[...]
    predicted = pred[...]
    weighted = (weight * weight * predicted).astype(BF16).astype(F32)
    curvature = total(predicted * weighted) + beta_reg * total(d_own * bent)
    pred[...] = weighted
    backward_rows(starts, order, cols, sens, pred, spread)
    write_payload(out, spread, curvature)


def gathered_sum(recv):
    def owner(o, acc):
        return acc + recv[o].astype(F32)

    return lax.fori_loop(0, GROUP_DEVS, owner, jnp.zeros((CELL_ROWS + EXTRA, 128), F32))


def broadcast_out(out, value):
    half = value.astype(BF16)

    def owner(o, _):
        out[o] = half
        return 0

    lax.fori_loop(0, GROUP_DEVS, owner, 0)


def right_side_kernel(recv, bent, r_out, out):
    sums = gathered_sum(recv)
    r = -(sums[:CELL_ROWS] + beta_reg * bent[...])
    r_out[...] = r
    broadcast_out(out, r)


def update_kernel(first_step, last_step, recv, bent, direction, residual, update, norm, u_out, r_out, *out):
    sums = gathered_sum(recv)
    curvature = total(sums[CELL_ROWS : CELL_ROWS + 8])
    alpha = norm[0:1, 0:1] / curvature
    d = direction[...]
    u_out[...] = alpha * d if first_step else update[...] + alpha * d
    r = residual[...] - alpha * (sums[:CELL_ROWS] + beta_reg * bent[...])
    r_out[...] = r
    if not last_step:
        broadcast_out(out[0], r)


VM = pl.BlockSpec(memory_space=pltpu.VMEM)
SM = pl.BlockSpec(memory_space=pltpu.SMEM)
PARAMS = pltpu.CompilerParams(vmem_limit_bytes=30 << 20)


def cells_shape():
    return jax.ShapeDtypeStruct((CELL_ROWS, 128), F32)


def scratch():
    return [
        pltpu.VMEM((TABLE + 8, 128), F32),
        pltpu.VMEM((ROWS, 128, 128), F32),
        pltpu.VMEM((ROWS, 128), F32),
        pltpu.VMEM((TABLE + 8, 128), F32),
        pltpu.VMEM((CELL_ROWS + 16, 128), F32),
    ]


def row_lists(block_rows, block_cols):
    blocks = block_rows.shape[0]
    longest = blocks + ROWS * (UNROLL - 1)
    ids = jnp.arange(blocks, dtype=jnp.int32)
    rows = jnp.arange(ROWS, dtype=jnp.int32)
    counts = jnp.sum((block_rows[None, :] == rows[:, None]).astype(jnp.int32), axis=1)
    padded = (counts + UNROLL - 1) // UNROLL * UNROLL
    starts = jnp.sum(
        jnp.where(rows[None, :] < jnp.arange(ROWS + 1, dtype=jnp.int32)[:, None], padded[None, :], 0), axis=1
    )
    earlier = (block_rows[None, :] == block_rows[:, None]) & (ids[None, :] < ids[:, None])
    lower = jnp.where(rows[None, :] < block_rows[:, None], padded[None, :], 0)
    place = jnp.sum(earlier.astype(jnp.int32), axis=1) + jnp.sum(lower, axis=1)
    hit = place[None, :] == jnp.arange(longest, dtype=jnp.int32)[:, None]
    order = jnp.sum(jnp.where(hit, ids[None, :], 0), axis=1)
    cols = TABLE + jnp.sum(jnp.where(hit, block_cols[None, :] - TABLE, 0), axis=1)
    return starts, order, cols


def per_device(
    sens, block_rows, block_cols, neighbours, observed, data_weight, smallness, model, reference_model
):
    starts, order, cols = row_lists(block_rows, block_cols)
    me = lax.axis_index(AXES).astype(jnp.int32).reshape(1)
    nb = neighbours.reshape(6, CELL_ROWS, 128)
    observed = observed.reshape(ROWS, 128)
    data_weight = data_weight.reshape(ROWS, 128)
    small = smallness.reshape(CELL_ROWS, 128)
    model = model.reshape(CELL_ROWS, 128)
    diff = model - reference_model.reshape(CELL_ROWS, 128)

    def exchange(x):
        return lax.all_to_all(x, AXES, 0, 0, tiled=True)

    payload = jnp.concatenate([model, diff[:8], diff[-8:]], axis=0).astype(BF16)
    recv = exchange(jnp.broadcast_to(payload[None], (GROUP_DEVS, CELL_ROWS + 16, 128)))
    sent = jax.ShapeDtypeStruct((GROUP_DEVS, CELL_ROWS + EXTRA, 128), BF16)
    gather = jax.ShapeDtypeStruct((GROUP_DEVS, CELL_ROWS, 128), BF16)
    sens = pltpu.with_memory_space_constraint(sens, pltpu.VMEM)
    out, bent = pl.pallas_call(
        start_kernel,
        out_shape=(sent, cells_shape()),
        in_specs=[SM] * 4 + [VM] * 7,
        out_specs=(VM, VM),
        scratch_shapes=scratch(),
        compiler_params=PARAMS,
        name="start",
    )(starts, order, cols, me, sens, recv, diff, observed, data_weight, nb, small)
    residual, out = pl.pallas_call(
        right_side_kernel,
        out_shape=(cells_shape(), gather),
        in_specs=[VM] * 2,
        out_specs=(VM, VM),
        compiler_params=PARAMS,
        name="right_side",
    )(exchange(out), bent)
    direction = residual
    update = residual
    d_all = jnp.zeros((8, 128), F32)
    norm = jnp.zeros((8, 128), F32)
    for step in range(CG_STEPS):
        first, last = step == 0, step == CG_STEPS - 1
        out, bent, direction, d_all, norm = pl.pallas_call(
            functools.partial(step_kernel, first),
            out_shape=(
                sent,
                cells_shape(),
                cells_shape(),
                jax.ShapeDtypeStruct((TABLE, 128), F32),
                jax.ShapeDtypeStruct((8, 128), F32),
            ),
            in_specs=[SM] * 4 + [VM] * 9,
            out_specs=(VM,) * 5,
            scratch_shapes=scratch(),
            compiler_params=PARAMS,
            name="step",
        )(starts, order, cols, me, sens, exchange(out), residual, direction, d_all, norm, data_weight, nb, small)
        results = pl.pallas_call(
            functools.partial(update_kernel, first, last),
            out_shape=(cells_shape(), cells_shape()) + (() if last else (gather,)),
            in_specs=[VM] * 6,
            out_specs=(VM,) * (2 if last else 3),
            compiler_params=PARAMS,
            name="update",
        )(exchange(out), bent, direction, residual, update, norm)
        update, residual = results[:2]
        if not last:
            out = results[2]
    return update.reshape(-1), residual.reshape(-1)


def solution(mesh):
    own = P(AXES)
    part = P(("ref",) + AXES)
    in_specs = (P(AXES, None, None), own, own, P(None, AXES), own, own, own, part, part)
    return jax.shard_map(
        per_device, mesh=mesh, in_specs=in_specs, out_specs=(part, part), check_vma=False
    )
```

```python
import functools

import jax
import jax.numpy as jnp
from jax import lax
from jax.experimental import pallas as pl
from jax.experimental.pallas import tpu as pltpu
from jax.sharding import PartitionSpec as P

CG_STEPS = 3
beta_reg = 0.5

AXES = ("lines", "cells")
BLOCKS = 512
CHUNK = 128
BATCH = 16
GROUP_DEVS = 64
ROWS = 32
CELL_ROWS = 32
TABLE = GROUP_DEVS * CELL_ROWS
SLOTS = 16
EXTRA = 16
SENT_ROWS = SLOTS + EXTRA
F32 = jnp.float32
BF16 = jnp.bfloat16


def total(x):
    return jnp.sum(jnp.sum(x, axis=0, keepdims=True), axis=1, keepdims=True)


def smooth_from(win, nb_ref, small, offset):
    sub = lax.broadcasted_iota(jnp.int32, (8, 128), 0)
    pieces = []
    for g in range(CELL_ROWS // 8):
        acc = jnp.zeros((8, 128), F32)
        lanes = []
        deltas = []
        for k in range(6):
            index = nb_ref[k, pl.ds(8 * g, 8), :] - offset + 1024
            lanes.append(index & 127)
            deltas.append((index >> 7) - 8 * g - sub)
        for delta in range(17):
            source = win[pl.ds(8 * g + delta, 8), :]
            for k in range(6):
                picked = jnp.take_along_axis(source, lanes[k], axis=1, mode="promise_in_bounds")
                acc = acc + jnp.where(deltas[k] == delta, picked, 0.0)
        own = win[pl.ds(8 * g + 8, 8), :]
        pieces.append((small[pl.ds(8 * g, 8), :] + 6.0) * own - acc)
    return jnp.concatenate(pieces, axis=0)


def gather_columns(cols, tab, temp, lhs):
    def rows(g, _):
        for q in range(64):
            k = g * 64 + q
            temp[pl.ds(k, 1), :] = tab[pl.ds(cols[k], 1), :]
        return 0

    lax.fori_loop(0, BLOCKS // 64, rows, 0)
    lhs[...] = temp[...].astype(BF16)


def forward_blocks(sens, lhs, products, ready=None):
    def chunk(g, _):
        first = pl.multiple_of(g * CHUNK, CHUNK)
        if ready is not None:
            ready(g)
        for h in range(CHUNK // BATCH):
            base = first + h * BATCH
            right = sens[pl.ds(base, BATCH)].reshape(BATCH * 128, 128)
            out = lax.dot_general(
                lhs[pl.ds(base, BATCH), :], right, (((1,), (1,)), ((), ())), preferred_element_type=F32
            )
            for q in range(BATCH):
                products[pl.ds(base + q, 1), :] = out[q : q + 1, q * 128 : (q + 1) * 128]
        return 0

    lax.fori_loop(0, BLOCKS // CHUNK, chunk, 0)


def row_hot(rows):
    return (lax.broadcasted_iota(jnp.int32, (ROWS, BLOCKS), 0) == rows[...]).astype(BF16)


def sum_rows(hot, products):
    value = products[...]
    high = value.astype(BF16)
    rest = value - high.astype(F32)
    middle = rest.astype(BF16)
    low = (rest - middle.astype(F32)).astype(BF16)
    return (
        jnp.dot(hot, high, preferred_element_type=F32)
        + jnp.dot(hot, middle, preferred_element_type=F32)
        + jnp.dot(hot, low, preferred_element_type=F32)
    )


def backward_blocks(hot, weighted, slots, sens, lhs, spread):
    lhs[...] = lax.dot_general(
        hot, weighted, (((0,), (0,)), ((), ())), preferred_element_type=F32
    ).astype(BF16)
    spread[...] = jnp.zeros_like(spread)

    def chunk(g, _):
        first = pl.multiple_of(g * CHUNK, CHUNK)
        for h in range(CHUNK // BATCH):
            base = first + h * BATCH
            right = jnp.concatenate([sens[base + q] for q in range(BATCH)], axis=1)
            out = jnp.dot(lhs[pl.ds(base, BATCH), :], right, preferred_element_type=F32)
            for q in range(BATCH):
                spread[pl.ds(slots[base + q], 1), :] = out[q : q + 1, q * 128 : (q + 1) * 128]
        return 0

    lax.fori_loop(0, BLOCKS // CHUNK, chunk, 0)


def scalar_tile(scalar):
    high = scalar.astype(BF16).astype(F32)
    middle = (scalar - high).astype(BF16).astype(F32)
    low = scalar - high - middle
    sub = lax.broadcasted_iota(jnp.int32, (EXTRA, 128), 0)
    lane = lax.broadcasted_iota(jnp.int32, (EXTRA, 128), 1)
    place = sub * 128 + lane
    return jnp.where(
        place == 0, high, jnp.where(place == 1, middle, jnp.where(place == 2, low, 0.0))
    ).astype(BF16)


def write_payload(out, spread, tail_of):
    def owners(g, _):
        for q in range(8):
            o = g * 8 + q
            base = pl.multiple_of(o * SLOTS, SLOTS)
            out[o, pl.ds(0, SLOTS), :] = spread[pl.ds(base, SLOTS), :].astype(BF16)
            out[o, pl.ds(SLOTS, EXTRA), :] = tail_of(o)
        return 0

    lax.fori_loop(0, GROUP_DEVS // 8, owners, 0)


def start_kernel(
    cols, slots, me, sens_hbm, rows, recv, diff, observed, data_weight, nb, small, slot_hot,
    out, bent_out, temp, lhs, spread, win, tab, sens, sems,
):
    def part(g):
        span = pl.ds(pl.multiple_of(g * CHUNK, CHUNK), CHUNK)
        return pltpu.make_async_copy(sens_hbm.at[span], sens.at[span], sems.at[g])

    for g in range(BLOCKS // CHUNK):
        part(g).start()

    def owners(g, _):
        for q in range(8):
            o = g * 8 + q
            base = pl.multiple_of(o * CELL_ROWS, CELL_ROWS)
            tab[pl.ds(base, CELL_ROWS), :] = recv[o, pl.ds(0, CELL_ROWS), :].astype(F32)
        return 0

    lax.fori_loop(0, GROUP_DEVS // 8, owners, 0)
    mine = me[0]
    before = jnp.maximum(mine - 1, 0)
    after = jnp.minimum(mine + 1, GROUP_DEVS - 1)
    win[pl.ds(0, 8), :] = recv[before, pl.ds(CELL_ROWS, 16), :].astype(F32)[8:16]
    win[pl.ds(8, CELL_ROWS), :] = diff[...]
    win[pl.ds(8 + CELL_ROWS, 8), :] = recv[after, pl.ds(CELL_ROWS, 16), :].astype(F32)[0:8]
    bent_out[...] = smooth_from(win, nb, small, mine * (CELL_ROWS * 128))
    gather_columns(cols, tab, temp, lhs)
    forward_blocks(sens, lhs, temp, lambda g: part(g).wait())
    hot = row_hot(rows)
    weight = data_weight[...]
    misfit = weight * weight * (sum_rows(hot, temp) - observed[...])
    backward_blocks(hot, misfit.astype(BF16), slots, sens, lhs, spread)
    write_payload(out, spread, lambda o: slot_hot[o])


def step_kernel(
    first_step,
    cols, slots, me, sens, rows, recv, residual, direction, d_all_in, norm_in, data_weight, nb, small,
    out, bent_out, d_out, d_all_out, norm_out, temp, lhs, spread, win,
):
    def squares(g, acc):
        for q in range(8):
            r = recv[g * 8 + q].astype(F32)
            acc = acc + r * r
        return acc

    acc = lax.fori_loop(0, GROUP_DEVS // 8, squares, jnp.zeros((CELL_ROWS, 128), F32))
    norm = total(acc)
    norm_out[...] = jnp.broadcast_to(norm, (8, 128))
    beta = None if first_step else norm / norm_in[0:1, 0:1]

    def owners(g, _):
        for q in range(8):
            o = g * 8 + q
            base = pl.multiple_of(o * CELL_ROWS, CELL_ROWS)
            d = recv[o].astype(F32)
            if not first_step:
                d = d + beta * d_all_in[pl.ds(base, CELL_ROWS), :]
            d_all_out[pl.ds(base, CELL_ROWS), :] = d
        return 0

    lax.fori_loop(0, GROUP_DEVS // 8, owners, 0)
    d_own = residual[...]
    if not first_step:
        d_own = d_own + beta * direction[...]
    d_out[...] = d_own
    mine = me[0]
    base = mine * CELL_ROWS
    before = pl.multiple_of(jnp.maximum(base - 8, 0), 8)
    after = pl.multiple_of(jnp.minimum(base + CELL_ROWS, TABLE - 8), 8)
    win[pl.ds(0, 8), :] = d_all_out[pl.ds(before, 8), :]
    win[pl.ds(8, CELL_ROWS), :] = d_own
    win[pl.ds(8 + CELL_ROWS, 8), :] = d_all_out[pl.ds(after, 8), :]
    bent = smooth_from(win, nb, small, mine * (CELL_ROWS * 128))
    bent_out[...] = bent
    gather_columns(cols, d_all_out, temp, lhs)
    forward_blocks(sens, lhs, temp)
    hot = row_hot(rows)
    weight = data_weight[...]
    predicted = sum_rows(hot, temp)
    weighted = (weight * weight * predicted).astype(BF16)
    curvature = total(predicted * weighted.astype(F32)) + beta_reg * total(d_own * bent)
    backward_blocks(hot, weighted, slots, sens, lhs, spread)
    tail = scalar_tile(curvature)
    write_payload(out, spread, lambda o: tail)


def gathered_sum(recv, pick):
    values = recv[:, 0:SLOTS, :].reshape(GROUP_DEVS * SLOTS, 128)
    return jnp.dot(pick, values, preferred_element_type=F32)


def broadcast_out(out, value):
    half = value.astype(BF16)

    def owners(g, _):
        for q in range(8):
            out[g * 8 + q] = half
        return 0

    lax.fori_loop(0, GROUP_DEVS // 8, owners, 0)


def right_side_kernel(recv, bent, r_out, out, pick_out):
    hot = recv[:, SLOTS : SLOTS + EXTRA, :].reshape(GROUP_DEVS * SLOTS, 128)
    pick = hot.astype(F32).T[:CELL_ROWS].astype(BF16)
    pick_out[...] = pick
    r = -(gathered_sum(recv, pick) + beta_reg * bent[...])
    r_out[...] = r
    broadcast_out(out, r)


def update_kernel(first_step, last_step, recv, pick, bent, direction, residual, update, norm, u_out, r_out, *out):
    sums = gathered_sum(recv, pick[...])

    def tails(g, acc):
        for q in range(8):
            acc = acc + recv[g * 8 + q, pl.ds(SLOTS, EXTRA), :].astype(F32)
        return acc

    curvature = total(lax.fori_loop(0, GROUP_DEVS // 8, tails, jnp.zeros((EXTRA, 128), F32)))
    alpha = norm[0:1, 0:1] / curvature
    d = direction[...]
    u_out[...] = alpha * d if first_step else update[...] + alpha * d
    r = residual[...] - alpha * (sums + beta_reg * bent[...])
    r_out[...] = r
    if not last_step:
        broadcast_out(out[0], r)


VM = pl.BlockSpec(memory_space=pltpu.VMEM)
SM = pl.BlockSpec(memory_space=pltpu.SMEM)
PARAMS = pltpu.CompilerParams(vmem_limit_bytes=12 << 20)


def cells_shape():
    return jax.ShapeDtypeStruct((CELL_ROWS, 128), F32)


def scratch():
    return [
        pltpu.VMEM((BLOCKS, 128), F32),
        pltpu.VMEM((BLOCKS, 128), BF16),
        pltpu.VMEM((GROUP_DEVS * SLOTS, 128), F32),
        pltpu.VMEM((CELL_ROWS + 16, 128), F32),
    ]


def slot_lists(block_cols):
    ids = jnp.arange(BLOCKS, dtype=jnp.int32)
    owners = block_cols // CELL_ROWS
    shared = (owners[None, :] == owners[:, None]) & (ids[None, :] < ids[:, None])
    slots = owners * SLOTS + jnp.sum(shared.astype(jnp.int32), axis=1)
    taken = slots[None, :] == jnp.arange(GROUP_DEVS * SLOTS, dtype=jnp.int32)[:, None]
    cell = jnp.sum(jnp.where(taken, (block_cols % CELL_ROWS)[None, :] + 1, 0), axis=1) - 1
    hot = (cell[:, None] == jnp.arange(128, dtype=jnp.int32)[None, :]).astype(BF16)
    return slots, hot.reshape(GROUP_DEVS, SLOTS, 128)


def per_device(
    sens, block_rows, block_cols, neighbours, observed, data_weight, smallness, model, reference_model
):
    cols = block_cols
    slots, slot_hot = slot_lists(block_cols)
    rows = block_rows.reshape(1, BLOCKS)
    me = lax.axis_index(AXES).astype(jnp.int32).reshape(1)
    nb = neighbours.reshape(6, CELL_ROWS, 128)
    observed = observed.reshape(ROWS, 128)
    data_weight = data_weight.reshape(ROWS, 128)
    small = smallness.reshape(CELL_ROWS, 128)
    model = model.reshape(CELL_ROWS, 128)
    diff = model - reference_model.reshape(CELL_ROWS, 128)

    def exchange(x):
        return lax.all_to_all(x, AXES, 0, 0, tiled=True)

    payload = jnp.concatenate([model, diff[:8], diff[-8:]], axis=0).astype(BF16)
    recv = exchange(jnp.broadcast_to(payload[None], (GROUP_DEVS, CELL_ROWS + 16, 128)))
    sent = jax.ShapeDtypeStruct((GROUP_DEVS, SENT_ROWS, 128), BF16)
    gather = jax.ShapeDtypeStruct((GROUP_DEVS, CELL_ROWS, 128), BF16)
    out, bent = pl.pallas_call(
        start_kernel,
        out_shape=(sent, cells_shape()),
        in_specs=[SM] * 3 + [pl.BlockSpec(memory_space=pltpu.HBM)] + [VM] * 8,
        out_specs=(VM, VM),
        scratch_shapes=scratch()
        + [
            pltpu.VMEM((TABLE, 128), F32),
            pltpu.VMEM((BLOCKS, 128, 128), BF16),
            pltpu.SemaphoreType.DMA((BLOCKS // CHUNK,)),
        ],
        compiler_params=pltpu.CompilerParams(vmem_limit_bytes=26 << 20),
        name="start",
    )(cols, slots, me, pltpu.with_memory_space_constraint(sens, pltpu.HBM), rows, recv, diff, observed, data_weight, nb, small, slot_hot)
    sens = pltpu.with_memory_space_constraint(sens, pltpu.VMEM)
    residual, out, pick = pl.pallas_call(
        right_side_kernel,
        out_shape=(cells_shape(), gather, jax.ShapeDtypeStruct((CELL_ROWS, GROUP_DEVS * SLOTS), BF16)),
        in_specs=[VM] * 2,
        out_specs=(VM,) * 3,
        compiler_params=PARAMS,
        name="right_side",
    )(exchange(out), bent)
    direction = residual
    update = residual
    d_all = jnp.zeros((8, 128), F32)
    norm = jnp.zeros((8, 128), F32)
    for step in range(CG_STEPS):
        first, last = step == 0, step == CG_STEPS - 1
        out, bent, direction, d_all, norm = pl.pallas_call(
            functools.partial(step_kernel, first),
            out_shape=(
                sent,
                cells_shape(),
                cells_shape(),
                jax.ShapeDtypeStruct((TABLE, 128), F32),
                jax.ShapeDtypeStruct((8, 128), F32),
            ),
            in_specs=[SM] * 3 + [VM] * 10,
            out_specs=(VM,) * 5,
            scratch_shapes=scratch(),
            compiler_params=PARAMS,
            name="step",
        )(cols, slots, me, sens, rows, exchange(out), residual, direction, d_all, norm, data_weight, nb, small)
        results = pl.pallas_call(
            functools.partial(update_kernel, first, last),
            out_shape=(cells_shape(), cells_shape()) + (() if last else (gather,)),
            in_specs=[VM] * 7,
            out_specs=(VM,) * (2 if last else 3),
            compiler_params=PARAMS,
            name="update",
        )(exchange(out), pick, bent, direction, residual, update, norm)
        update, residual = results[:2]
        if not last:
            out = results[2]
    return update.reshape(-1), residual.reshape(-1)


def solution(mesh):
    own = P(AXES)
    part = P(("ref",) + AXES)
    in_specs = (P(AXES, None, None), own, own, P(None, AXES), own, own, own, part, part)
    return jax.shard_map(
        per_device, mesh=mesh, in_specs=in_specs, out_specs=(part, part), check_vma=False
    )
```

```python
import functools

import jax
import jax.numpy as jnp
from jax import lax
from jax.experimental import pallas as pl
from jax.experimental.pallas import tpu as pltpu
from jax.sharding import PartitionSpec as P

CG_STEPS = 3
beta_reg = 0.5

AXES = ("lines", "cells")
BLOCKS = 512
CHUNK = 128
BATCH = 16
GROUP_DEVS = 64
ROWS = 32
CELL_ROWS = 32
TABLE = GROUP_DEVS * CELL_ROWS
SLOTS = 16
EXTRA = 16
SENT_ROWS = SLOTS + EXTRA
F32 = jnp.float32
BF16 = jnp.bfloat16


def total(x):
    return jnp.sum(jnp.sum(x, axis=0, keepdims=True), axis=1, keepdims=True)


def smooth_group(g, win, nb_ref, small, offset, out):
    first = pl.multiple_of(g * 8, 8)
    sub = lax.broadcasted_iota(jnp.int32, (8, 128), 0)
    acc = jnp.zeros((8, 128), F32)
    lanes = []
    deltas = []
    for k in range(6):
        index = nb_ref[k, pl.ds(first, 8), :] - offset + 1024
        lanes.append(index & 127)
        deltas.append((index >> 7) - first - sub)
    for delta in range(17):
        source = win[pl.ds(first + delta, 8), :]
        for k in range(6):
            picked = jnp.take_along_axis(source, lanes[k], axis=1, mode="promise_in_bounds")
            acc = acc + jnp.where(deltas[k] == delta, picked, 0.0)
    own = win[pl.ds(first + 8, 8), :]
    out[pl.ds(first, 8), :] = (small[pl.ds(first, 8), :] + 6.0) * own - acc


def forward_blocks(flipped, cols, tab, temp, products, beside, flip=None):
    def chunk(g, _):
        first = pl.multiple_of(g * CHUNK, CHUNK)
        if flip is not None:
            sens, wait = flip
            wait(g)
        beside(g)
        for h in range(CHUNK // BATCH):
            base = first + h * BATCH
            for q in range(BATCH):
                temp[pl.ds(base + q, 1), :] = tab[pl.ds(cols[base + q], 1), :]
            left = temp[pl.ds(base, BATCH), :].astype(BF16)
            if flip is not None:
                blocks = [sens[base + q].T for q in range(BATCH)]
                for q in range(BATCH):
                    flipped[base + q] = blocks[q]
            else:
                blocks = [flipped[base + q] for q in range(BATCH)]
            out = jnp.dot(left, jnp.concatenate(blocks, axis=1), preferred_element_type=F32)
            for q in range(BATCH):
                products[pl.ds(base + q, 1), :] = out[q : q + 1, q * 128 : (q + 1) * 128]
        return 0

    lax.fori_loop(0, BLOCKS // CHUNK, chunk, 0)


def row_hot(rows):
    return (lax.broadcasted_iota(jnp.int32, (ROWS, BLOCKS), 0) == rows[...]).astype(BF16)


def sum_rows(hot, products):
    value = products[...]
    high = value.astype(BF16)
    rest = value - high.astype(F32)
    middle = rest.astype(BF16)
    low = (rest - middle.astype(F32)).astype(BF16)
    return (
        jnp.dot(hot, high, preferred_element_type=F32)
        + jnp.dot(hot, middle, preferred_element_type=F32)
        + jnp.dot(hot, low, preferred_element_type=F32)
    )


def backward_blocks(hot, weighted, slots, sens, lhs, spread):
    lhs[...] = lax.dot_general(
        hot, weighted, (((0,), (0,)), ((), ())), preferred_element_type=F32
    ).astype(BF16)
    spread[...] = jnp.zeros_like(spread)

    def chunk(g, _):
        first = pl.multiple_of(g * CHUNK, CHUNK)
        for h in range(CHUNK // BATCH):
            base = first + h * BATCH
            right = jnp.concatenate([sens[base + q] for q in range(BATCH)], axis=1)
            out = jnp.dot(lhs[pl.ds(base, BATCH), :], right, preferred_element_type=F32)
            for q in range(BATCH):
                spread[pl.ds(slots[base + q], 1), :] = out[q : q + 1, q * 128 : (q + 1) * 128]
        return 0

    lax.fori_loop(0, BLOCKS // CHUNK, chunk, 0)


def scalar_tile(scalar):
    high = scalar.astype(BF16).astype(F32)
    middle = (scalar - high).astype(BF16).astype(F32)
    low = scalar - high - middle
    sub = lax.broadcasted_iota(jnp.int32, (EXTRA, 128), 0)
    lane = lax.broadcasted_iota(jnp.int32, (EXTRA, 128), 1)
    place = sub * 128 + lane
    return jnp.where(
        place == 0, high, jnp.where(place == 1, middle, jnp.where(place == 2, low, 0.0))
    ).astype(BF16)


def write_payload(out, spread, tail_of):
    def owners(g, _):
        for q in range(8):
            o = g * 8 + q
            base = pl.multiple_of(o * SLOTS, SLOTS)
            out[o, pl.ds(0, SLOTS), :] = spread[pl.ds(base, SLOTS), :].astype(BF16)
            out[o, pl.ds(SLOTS, EXTRA), :] = tail_of(o)
        return 0

    lax.fori_loop(0, GROUP_DEVS // 8, owners, 0)


def model_kernel(model, reference_model, diff_out, out):
    diff = model[...] - reference_model[...]
    diff_out[...] = diff
    half = jnp.concatenate([model[...], diff[:8], diff[-8:]], axis=0).astype(BF16)

    def owners(g, _):
        for q in range(8):
            out[g * 8 + q] = half
        return 0

    lax.fori_loop(0, GROUP_DEVS // 8, owners, 0)


def start_kernel(
    cols, slots, me, sens_hbm, rows, recv, diff, observed, data_weight, nb, small, slot_hot,
    out, bent_out, sens, flipped, temp, products, lhs, spread, win, tab, sems,
):
    def part(g):
        span = pl.ds(pl.multiple_of(g * CHUNK, CHUNK), CHUNK)
        return pltpu.make_async_copy(sens_hbm.at[span], sens.at[span], sems.at[g])

    for g in range(BLOCKS // CHUNK):
        part(g).start()

    def owners(g, _):
        for q in range(8):
            o = g * 8 + q
            base = pl.multiple_of(o * CELL_ROWS, CELL_ROWS)
            tab[pl.ds(base, CELL_ROWS), :] = recv[o, pl.ds(0, CELL_ROWS), :].astype(F32)
        return 0

    lax.fori_loop(0, GROUP_DEVS // 8, owners, 0)
    mine = me[0]
    before = jnp.maximum(mine - 1, 0)
    after = jnp.minimum(mine + 1, GROUP_DEVS - 1)
    win[pl.ds(0, 8), :] = recv[before, pl.ds(CELL_ROWS, 16), :].astype(F32)[8:16]
    win[pl.ds(8, CELL_ROWS), :] = diff[...]
    win[pl.ds(8 + CELL_ROWS, 8), :] = recv[after, pl.ds(CELL_ROWS, 16), :].astype(F32)[0:8]
    beside = functools.partial(
        smooth_group, win=win, nb_ref=nb, small=small, offset=mine * (CELL_ROWS * 128), out=bent_out
    )
    forward_blocks(flipped, cols, tab, temp, products, beside, (sens, lambda g: part(g).wait()))
    hot = row_hot(rows)
    weight = data_weight[...]
    misfit = weight * weight * (sum_rows(hot, products) - observed[...])
    backward_blocks(hot, misfit.astype(BF16), slots, sens, lhs, spread)
    write_payload(out, spread, lambda o: slot_hot[o])


def step_kernel(
    first_step,
    cols, slots, me, sens, flipped, rows, recv, residual, direction, d_all_in, norm_in, data_weight, nb, small,
    out, bent_out, d_out, d_all_out, norm_out, temp, products, lhs, spread, win,
):
    def squares(g, acc):
        for q in range(8):
            r = recv[g * 8 + q].astype(F32)
            acc = acc + r * r
        return acc

    acc = lax.fori_loop(0, GROUP_DEVS // 8, squares, jnp.zeros((CELL_ROWS, 128), F32))
    norm = total(acc)
    norm_out[...] = jnp.broadcast_to(norm, (8, 128))
    beta = None if first_step else norm / norm_in[0:1, 0:1]

    def owners(g, _):
        for q in range(8):
            o = g * 8 + q
            base = pl.multiple_of(o * CELL_ROWS, CELL_ROWS)
            d = recv[o].astype(F32)
            if not first_step:
                d = d + beta * d_all_in[pl.ds(base, CELL_ROWS), :]
            d_all_out[pl.ds(base, CELL_ROWS), :] = d
        return 0

    lax.fori_loop(0, GROUP_DEVS // 8, owners, 0)
    d_own = residual[...]
    if not first_step:
        d_own = d_own + beta * direction[...]
    d_out[...] = d_own
    mine = me[0]
    base = mine * CELL_ROWS
    before = pl.multiple_of(jnp.maximum(base - 8, 0), 8)
    after = pl.multiple_of(jnp.minimum(base + CELL_ROWS, TABLE - 8), 8)
    win[pl.ds(0, 8), :] = d_all_out[pl.ds(before, 8), :]
    win[pl.ds(8, CELL_ROWS), :] = d_own
    win[pl.ds(8 + CELL_ROWS, 8), :] = d_all_out[pl.ds(after, 8), :]
    beside = functools.partial(
        smooth_group, win=win, nb_ref=nb, small=small, offset=mine * (CELL_ROWS * 128), out=bent_out
    )
    forward_blocks(flipped, cols, d_all_out, temp, products, beside)
    hot = row_hot(rows)
    weight = data_weight[...]
    predicted = sum_rows(hot, products)
    weighted = (weight * weight * predicted).astype(BF16)
    curvature = total(predicted * weighted.astype(F32)) + beta_reg * total(d_own * bent_out[...])
    backward_blocks(hot, weighted, slots, sens, lhs, spread)
    tail = scalar_tile(curvature)
    write_payload(out, spread, lambda o: tail)


def gathered_sum(recv, pick):
    values = recv[:, 0:SLOTS, :].reshape(GROUP_DEVS * SLOTS, 128)
    return jnp.dot(pick, values, preferred_element_type=F32)


def broadcast_out(out, value):
    half = value.astype(BF16)

    def owners(g, _):
        for q in range(8):
            out[g * 8 + q] = half
        return 0

    lax.fori_loop(0, GROUP_DEVS // 8, owners, 0)


def right_side_kernel(recv, bent, r_out, out, pick_out):
    hot = recv[:, SLOTS : SLOTS + EXTRA, :].reshape(GROUP_DEVS * SLOTS, 128)
    pick = hot.astype(F32).T[:CELL_ROWS].astype(BF16)
    pick_out[...] = pick
    r = -(gathered_sum(recv, pick) + beta_reg * bent[...])
    r_out[...] = r
    broadcast_out(out, r)


def update_kernel(first_step, last_step, recv, pick, bent, direction, residual, update, norm, u_out, r_out, *out):
    sums = gathered_sum(recv, pick[...])

    def tails(g, acc):
        for q in range(8):
            acc = acc + recv[g * 8 + q, pl.ds(SLOTS, EXTRA), :].astype(F32)
        return acc

    curvature = total(lax.fori_loop(0, GROUP_DEVS // 8, tails, jnp.zeros((EXTRA, 128), F32)))
    alpha = norm[0:1, 0:1] / curvature
    d = direction[...]
    u_out[...] = alpha * d if first_step else update[...] + alpha * d
    r = residual[...] - alpha * (sums + beta_reg * bent[...])
    r_out[...] = r
    if not last_step:
        broadcast_out(out[0], r)


VM = pl.BlockSpec(memory_space=pltpu.VMEM)
SM = pl.BlockSpec(memory_space=pltpu.SMEM)
PARAMS = pltpu.CompilerParams(vmem_limit_bytes=12 << 20)


def cells_shape():
    return jax.ShapeDtypeStruct((CELL_ROWS, 128), F32)


def scratch():
    return [
        pltpu.VMEM((BLOCKS, 128), F32),
        pltpu.VMEM((BLOCKS, 128), F32),
        pltpu.VMEM((BLOCKS, 128), BF16),
        pltpu.VMEM((GROUP_DEVS * SLOTS, 128), F32),
        pltpu.VMEM((CELL_ROWS + 16, 128), F32),
    ]


def slot_lists(block_cols):
    ids = jnp.arange(BLOCKS, dtype=jnp.int32)
    owners = block_cols // CELL_ROWS
    shared = (owners[None, :] == owners[:, None]) & (ids[None, :] < ids[:, None])
    slots = owners * SLOTS + jnp.sum(shared.astype(jnp.int32), axis=1)
    taken = slots[None, :] == jnp.arange(GROUP_DEVS * SLOTS, dtype=jnp.int32)[:, None]
    cell = jnp.sum(jnp.where(taken, (block_cols % CELL_ROWS)[None, :] + 1, 0), axis=1) - 1
    hot = (cell[:, None] == jnp.arange(128, dtype=jnp.int32)[None, :]).astype(BF16)
    return slots, hot.reshape(GROUP_DEVS, SLOTS, 128)


def per_device(
    sens, block_rows, block_cols, neighbours, observed, data_weight, smallness, model, reference_model
):
    cols = block_cols
    slots, slot_hot = slot_lists(block_cols)
    rows = block_rows.reshape(1, BLOCKS)
    me = lax.axis_index(AXES).astype(jnp.int32).reshape(1)
    nb = neighbours.reshape(6, CELL_ROWS, 128)
    observed = observed.reshape(ROWS, 128)
    data_weight = data_weight.reshape(ROWS, 128)
    small = smallness.reshape(CELL_ROWS, 128)
    model = model.reshape(CELL_ROWS, 128)

    def exchange(x):
        return lax.all_to_all(x, AXES, 0, 0, tiled=True)

    diff, out = pl.pallas_call(
        model_kernel,
        out_shape=(cells_shape(), jax.ShapeDtypeStruct((GROUP_DEVS, CELL_ROWS + 16, 128), BF16)),
        in_specs=[VM] * 2,
        out_specs=(VM, VM),
        compiler_params=PARAMS,
        name="model",
    )(model, reference_model.reshape(CELL_ROWS, 128))
    recv = exchange(out)
    sent = jax.ShapeDtypeStruct((GROUP_DEVS, SENT_ROWS, 128), BF16)
    gather = jax.ShapeDtypeStruct((GROUP_DEVS, CELL_ROWS, 128), BF16)
    out, bent, kept, flipped = pl.pallas_call(
        start_kernel,
        out_shape=(sent, cells_shape(), pltpu.VMEM(sens.shape, BF16), pltpu.VMEM(sens.shape, BF16)),
        in_specs=[SM] * 3 + [pl.BlockSpec(memory_space=pltpu.HBM)] + [VM] * 8,
        out_specs=(VM,) * 4,
        scratch_shapes=scratch()
        + [
            pltpu.VMEM((TABLE, 128), F32),
            pltpu.SemaphoreType.DMA((BLOCKS // CHUNK,)),
        ],
        compiler_params=pltpu.CompilerParams(vmem_limit_bytes=12 << 20),
        name="start",
    )(cols, slots, me, pltpu.with_memory_space_constraint(sens, pltpu.HBM), rows, recv, diff, observed, data_weight, nb, small, slot_hot)
    kept = pltpu.with_memory_space_constraint(kept, pltpu.VMEM)
    flipped = pltpu.with_memory_space_constraint(flipped, pltpu.VMEM)
    residual, out, pick = pl.pallas_call(
        right_side_kernel,
        out_shape=(cells_shape(), gather, jax.ShapeDtypeStruct((CELL_ROWS, GROUP_DEVS * SLOTS), BF16)),
        in_specs=[VM] * 2,
        out_specs=(VM,) * 3,
        compiler_params=PARAMS,
        name="right_side",
    )(exchange(out), bent)
    direction = residual
    update = residual
    d_all = jnp.zeros((8, 128), F32)
    norm = jnp.zeros((8, 128), F32)
    for step in range(CG_STEPS):
        first, last = step == 0, step == CG_STEPS - 1
        out, bent, direction, d_all, norm = pl.pallas_call(
            functools.partial(step_kernel, first),
            out_shape=(
                sent,
                cells_shape(),
                cells_shape(),
                jax.ShapeDtypeStruct((TABLE, 128), F32),
                jax.ShapeDtypeStruct((8, 128), F32),
            ),
            in_specs=[SM] * 3 + [VM] * 11,
            out_specs=(VM,) * 5,
            scratch_shapes=scratch(),
            compiler_params=PARAMS,
            name="step",
        )(cols, slots, me, kept, flipped, rows, exchange(out), residual, direction, d_all, norm, data_weight, nb, small)
        results = pl.pallas_call(
            functools.partial(update_kernel, first, last),
            out_shape=(cells_shape(), cells_shape()) + (() if last else (gather,)),
            in_specs=[VM] * 7,
            out_specs=(VM,) * (2 if last else 3),
            compiler_params=PARAMS,
            name="update",
        )(exchange(out), pick, bent, direction, residual, update, norm)
        update, residual = results[:2]
        if not last:
            out = results[2]
    return update.reshape(-1), residual.reshape(-1)


def solution(mesh):
    own = P(AXES)
    part = P(("ref",) + AXES)
    in_specs = (P(AXES, None, None), own, own, P(None, AXES), own, own, own, part, part)
    return jax.shard_map(
        per_device, mesh=mesh, in_specs=in_specs, out_specs=(part, part), check_vma=False
    )
```

```python
import functools

import jax
import jax.numpy as jnp
from jax import lax
from jax.experimental import pallas as pl
from jax.experimental.pallas import tpu as pltpu
from jax.sharding import PartitionSpec as P

CG_STEPS = 3
beta_reg = 0.5

AXES = ("lines", "cells")
BLOCKS = 512
CHUNK = 256
START_CHUNK = 256
PARTS = BLOCKS // START_CHUNK
BATCH = 16
GROUP_DEVS = 64
ROWS = 32
CELL_ROWS = 32
TABLE = GROUP_DEVS * CELL_ROWS
SLOTS = 16
EXTRA = 8
F32 = jnp.float32
BF16 = jnp.bfloat16


def total(x):
    return jnp.sum(jnp.sum(x, axis=0, keepdims=True), axis=1, keepdims=True)


def smooth_group(g, win, nb_ref, small, offset, out):
    first = pl.multiple_of(g * 8, 8)
    sub = lax.broadcasted_iota(jnp.int32, (8, 128), 0)
    acc = jnp.zeros((8, 128), F32)
    lanes = []
    deltas = []
    for k in range(6):
        index = nb_ref[k, pl.ds(first, 8), :] - offset + 1024
        lanes.append(index & 127)
        deltas.append((index >> 7) - first - sub)
    for delta in range(17):
        source = win[pl.ds(first + delta, 8), :]
        for k in range(6):
            picked = jnp.take_along_axis(source, lanes[k], axis=1, mode="promise_in_bounds")
            acc = acc + jnp.where(deltas[k] == delta, picked, 0.0)
    own = win[pl.ds(first + 8, 8), :]
    out[pl.ds(first, 8), :] = (small[pl.ds(first, 8), :] + 6.0) * own - acc


def forward_blocks(flipped, cols, tab, temp, products, beside, flip=None):
    size = CHUNK if flip is None else START_CHUNK
    pieces = CELL_ROWS // 8 * size // BLOCKS

    def chunk(g, _):
        first = pl.multiple_of(g * size, size)
        if flip is not None:
            sens, wait = flip
            wait(g)
        for piece in range(pieces):
            beside(g * pieces + piece)
        for h in range(size // BATCH):
            base = first + h * BATCH
            for q in range(BATCH):
                temp[pl.ds(base + q, 1), :] = tab[pl.ds(cols[base + q], 1), :]
            left = temp[pl.ds(base, BATCH), :].astype(BF16)
            if flip is not None:
                blocks = [sens[base + q].T for q in range(BATCH)]
                for q in range(BATCH):
                    flipped[base + q] = blocks[q]
            else:
                blocks = [flipped[base + q] for q in range(BATCH)]
            out = jnp.dot(left, jnp.concatenate(blocks, axis=1), preferred_element_type=F32)
            for q in range(BATCH):
                products[pl.ds(base + q, 1), :] = out[q : q + 1, q * 128 : (q + 1) * 128]
        return 0

    lax.fori_loop(0, BLOCKS // size, chunk, 0)


def row_hot(rows):
    return (lax.broadcasted_iota(jnp.int32, (ROWS, BLOCKS), 0) == rows[...]).astype(BF16)


def sum_rows(hot, products):
    value = products[...]
    high = value.astype(BF16)
    rest = value - high.astype(F32)
    middle = rest.astype(BF16)
    low = (rest - middle.astype(F32)).astype(BF16)
    return (
        jnp.dot(hot, high, preferred_element_type=F32)
        + jnp.dot(hot, middle, preferred_element_type=F32)
        + jnp.dot(hot, low, preferred_element_type=F32)
    )


def backward_blocks(hot, weighted, slots, sens, lhs, spread):
    lhs[...] = lax.dot_general(
        hot, weighted, (((0,), (0,)), ((), ())), preferred_element_type=F32
    ).astype(BF16)
    spread[...] = jnp.zeros_like(spread)

    def chunk(g, _):
        first = pl.multiple_of(g * CHUNK, CHUNK)
        for h in range(CHUNK // BATCH):
            base = first + h * BATCH
            right = jnp.concatenate([sens[base + q] for q in range(BATCH)], axis=1)
            out = jnp.dot(lhs[pl.ds(base, BATCH), :], right, preferred_element_type=F32)
            for q in range(BATCH):
                spread[pl.ds(slots[base + q], 1), :] = out[q : q + 1, q * 128 : (q + 1) * 128]
        return 0

    lax.fori_loop(0, BLOCKS // CHUNK, chunk, 0)


def scalar_tile(scalar):
    high = scalar.astype(BF16).astype(F32)
    middle = (scalar - high).astype(BF16).astype(F32)
    low = scalar - high - middle
    sub = lax.broadcasted_iota(jnp.int32, (EXTRA, 128), 0)
    lane = lax.broadcasted_iota(jnp.int32, (EXTRA, 128), 1)
    place = sub * 128 + lane
    return jnp.where(
        place == 0, high, jnp.where(place == 1, middle, jnp.where(place == 2, low, 0.0))
    )


def write_payload(out, spread, tail_of):
    def owners(g, _):
        for q in range(8):
            o = g * 8 + q
            base = pl.multiple_of(o * SLOTS, SLOTS)
            out[o] = jnp.concatenate([spread[pl.ds(base, SLOTS), :], tail_of(o)], axis=0).astype(BF16)
        return 0

    lax.fori_loop(0, GROUP_DEVS // 8, owners, 0)


def model_kernel(model_hbm, reference_hbm, diff_out, out, model, reference_model, half, sems):
    first = pltpu.make_async_copy(model_hbm, model, sems.at[0])
    second = pltpu.make_async_copy(reference_hbm, reference_model, sems.at[1])
    first.start()
    second.start()
    first.wait()
    second.wait()
    diff = model[...] - reference_model[...]
    diff_out[...] = diff
    payload = jnp.concatenate([model[...], diff[:8], diff[-8:]], axis=0).astype(BF16)
    for q in range(8):
        half[q] = payload
    sends = [
        pltpu.make_async_copy(half, out.at[pl.ds(8 * g, 8)], sems.at[2 + g]) for g in range(GROUP_DEVS // 8)
    ]
    for send in sends:
        send.start()
    for send in sends:
        send.wait()


def start_kernel(
    cols, slots, me, sens_hbm, recv, *refs,
):
    given, (out, bent_out, sens, flipped), held = refs[:7], refs[7:11], refs[11:18]
    temp, products, lhs, spread, win, tab, sems, held_sems = refs[18:]
    diff, small, nb, rows, observed, data_weight, slot_hot = held
    copies = [
        pltpu.make_async_copy(source, target, held_sems.at[i])
        for i, (source, target) in enumerate(zip(given, held))
    ]
    for copy in copies:
        copy.start()

    def part(g):
        span = pl.ds(pl.multiple_of(g * START_CHUNK, START_CHUNK), START_CHUNK)
        return pltpu.make_async_copy(sens_hbm.at[span], sens.at[span], sems.at[g])

    for g in range(PARTS):
        part(g).start()
    for copy in copies:
        copy.wait()

    def owners(g, _):
        for q in range(8):
            o = g * 8 + q
            base = pl.multiple_of(o * CELL_ROWS, CELL_ROWS)
            tab[pl.ds(base, CELL_ROWS), :] = recv[o, pl.ds(0, CELL_ROWS), :].astype(F32)
        return 0

    lax.fori_loop(0, GROUP_DEVS // 8, owners, 0)
    mine = me[0]
    before = jnp.maximum(mine - 1, 0)
    after = jnp.minimum(mine + 1, GROUP_DEVS - 1)
    win[pl.ds(0, 8), :] = recv[before, pl.ds(CELL_ROWS, 16), :].astype(F32)[8:16]
    win[pl.ds(8, CELL_ROWS), :] = diff[...]
    win[pl.ds(8 + CELL_ROWS, 8), :] = recv[after, pl.ds(CELL_ROWS, 16), :].astype(F32)[0:8]
    beside = functools.partial(
        smooth_group, win=win, nb_ref=nb, small=small, offset=mine * (CELL_ROWS * 128), out=bent_out
    )
    forward_blocks(flipped, cols, tab, temp, products, beside, (sens, lambda g: part(g).wait()))
    hot = row_hot(rows)
    weight = data_weight[...]
    misfit = weight * weight * (sum_rows(hot, products) - observed[...])
    backward_blocks(hot, misfit.astype(BF16), slots, sens, lhs, spread)
    write_payload(out, spread, lambda o: slot_hot[o].astype(F32))


def step_kernel(
    first_step,
    cols, slots, me, sens, flipped, rows, recv, residual, direction, d_all_in, norm_in, data_weight, nb, small,
    out, bent_out, d_out, norm_out, d_all_out, temp, products, lhs, spread, win,
):
    def squares(g, acc):
        for q in range(8):
            r = recv[g * 8 + q].astype(F32)
            acc = acc + r * r
        return acc

    acc = lax.fori_loop(0, GROUP_DEVS // 8, squares, jnp.zeros((CELL_ROWS, 128), F32))
    norm = total(acc)
    norm_out[...] = jnp.broadcast_to(norm, (8, 128))
    beta = None if first_step else norm / norm_in[0:1, 0:1]

    def owners(g, _):
        for q in range(8):
            o = g * 8 + q
            base = pl.multiple_of(o * CELL_ROWS, CELL_ROWS)
            d = recv[o].astype(F32)
            if not first_step:
                d = d + beta * d_all_in[pl.ds(base, CELL_ROWS), :]
            d_all_out[pl.ds(base, CELL_ROWS), :] = d
        return 0

    lax.fori_loop(0, GROUP_DEVS // 8, owners, 0)
    d_own = residual[...]
    if not first_step:
        d_own = d_own + beta * direction[...]
    d_out[...] = d_own
    mine = me[0]
    base = mine * CELL_ROWS
    before = pl.multiple_of(jnp.maximum(base - 8, 0), 8)
    after = pl.multiple_of(jnp.minimum(base + CELL_ROWS, TABLE - 8), 8)
    win[pl.ds(0, 8), :] = d_all_out[pl.ds(before, 8), :]
    win[pl.ds(8, CELL_ROWS), :] = d_own
    win[pl.ds(8 + CELL_ROWS, 8), :] = d_all_out[pl.ds(after, 8), :]
    beside = functools.partial(
        smooth_group, win=win, nb_ref=nb, small=small, offset=mine * (CELL_ROWS * 128), out=bent_out
    )
    forward_blocks(flipped, cols, d_all_out, temp, products, beside)
    hot = row_hot(rows)
    weight = data_weight[...]
    predicted = sum_rows(hot, products)
    weighted = (weight * weight * predicted).astype(BF16)
    curvature = total(predicted * weighted.astype(F32)) + beta_reg * total(d_own * bent_out[...])
    backward_blocks(hot, weighted, slots, sens, lhs, spread)
    tail = scalar_tile(curvature)
    write_payload(out, spread, lambda o: tail)


def gathered_sum(recv, pick):
    values = recv[:, 0:SLOTS, :].reshape(GROUP_DEVS * SLOTS, 128)
    return jnp.dot(pick, values, preferred_element_type=F32)


def broadcast_out(out, value):
    half = value.astype(BF16)

    def owners(g, _):
        for q in range(8):
            out[g * 8 + q] = half
        return 0

    lax.fori_loop(0, GROUP_DEVS // 8, owners, 0)


def right_side_kernel(recv, bent, r_out, out, pick_out):
    hot = recv[:, SLOTS : 2 * SLOTS, :].reshape(GROUP_DEVS * SLOTS, 128)
    pick = hot.astype(F32).T[:CELL_ROWS].astype(BF16)
    pick_out[...] = pick
    r = -(gathered_sum(recv, pick) + beta_reg * bent[...])
    r_out[...] = r
    broadcast_out(out, r)


def update_kernel(first_step, last_step, recv, pick, bent, direction, residual, update, norm, u_out, r_out, *out):
    sums = gathered_sum(recv, pick[...])

    def tails(g, acc):
        for q in range(8):
            acc = acc + recv[g * 8 + q].astype(F32)[SLOTS:]
        return acc

    curvature = total(lax.fori_loop(0, GROUP_DEVS // 8, tails, jnp.zeros((EXTRA, 128), F32)))
    alpha = norm[0:1, 0:1] / curvature
    d = direction[...]
    u_out[...] = alpha * d if first_step else update[...] + alpha * d
    r = residual[...] - alpha * (sums + beta_reg * bent[...])
    r_out[...] = r
    if not last_step:
        broadcast_out(out[0], r)


VM = pl.BlockSpec(memory_space=pltpu.VMEM)
SM = pl.BlockSpec(memory_space=pltpu.SMEM)
HB = pl.BlockSpec(memory_space=pltpu.HBM)
PARAMS = pltpu.CompilerParams(vmem_limit_bytes=12 << 20)


def in_hbm(x):
    return pltpu.with_memory_space_constraint(x, pltpu.HBM)


def cells_shape():
    return jax.ShapeDtypeStruct((CELL_ROWS, 128), F32)


def scratch():
    return [
        pltpu.VMEM((BLOCKS, 128), F32),
        pltpu.VMEM((BLOCKS, 128), F32),
        pltpu.VMEM((BLOCKS, 128), BF16),
        pltpu.VMEM((GROUP_DEVS * SLOTS, 128), F32),
        pltpu.VMEM((CELL_ROWS + 16, 128), F32),
    ]


def slot_lists(block_cols):
    ids = jnp.arange(BLOCKS, dtype=jnp.int32)
    owners = block_cols // CELL_ROWS
    shared = (owners[None, :] == owners[:, None]) & (ids[None, :] < ids[:, None])
    slots = owners * SLOTS + jnp.sum(shared.astype(jnp.int32), axis=1)
    taken = slots[None, :] == jnp.arange(GROUP_DEVS * SLOTS, dtype=jnp.int32)[:, None]
    cell = jnp.sum(jnp.where(taken, (block_cols % CELL_ROWS)[None, :] + 1, 0), axis=1) - 1
    hot = (cell[:, None] == jnp.arange(128, dtype=jnp.int32)[None, :]).astype(BF16)
    return slots, hot.reshape(GROUP_DEVS, SLOTS, 128)


def per_device(
    sens, block_rows, block_cols, neighbours, observed, data_weight, smallness, model, reference_model
):
    cols = block_cols
    slots, slot_hot = slot_lists(block_cols)
    rows = block_rows.reshape(1, BLOCKS)
    me = lax.axis_index(AXES).astype(jnp.int32).reshape(1)
    nb = neighbours.reshape(6, CELL_ROWS, 128)
    observed = observed.reshape(ROWS, 128)
    data_weight = data_weight.reshape(ROWS, 128)
    small = smallness.reshape(CELL_ROWS, 128)
    model = model.reshape(CELL_ROWS, 128)

    def exchange(x):
        return lax.all_to_all(x, AXES, 0, 0, tiled=True)

    diff, out = pl.pallas_call(
        model_kernel,
        out_shape=(cells_shape(), pltpu.HBM((GROUP_DEVS, CELL_ROWS + 16, 128), BF16)),
        in_specs=[HB] * 2,
        out_specs=(VM, HB),
        scratch_shapes=[pltpu.VMEM((CELL_ROWS, 128), F32)] * 2
        + [pltpu.VMEM((8, CELL_ROWS + 16, 128), BF16), pltpu.SemaphoreType.DMA((2 + GROUP_DEVS // 8,))],
        compiler_params=PARAMS,
        name="model",
    )(in_hbm(model), in_hbm(reference_model.reshape(CELL_ROWS, 128)))
    recv = exchange(out)
    def sent(rows):
        return jax.ShapeDtypeStruct((GROUP_DEVS, SLOTS + rows, 128), BF16)

    gather = jax.ShapeDtypeStruct((GROUP_DEVS, CELL_ROWS, 128), BF16)
    given = (diff, small, nb, rows, observed, data_weight, slot_hot)
    out, bent, kept, flipped = pl.pallas_call(
        start_kernel,
        out_shape=(sent(SLOTS), cells_shape(), pltpu.VMEM(sens.shape, BF16), pltpu.VMEM(sens.shape, BF16)),
        in_specs=[SM] * 3 + [HB, VM] + [HB] * 7,
        out_specs=(VM,) * 4,
        scratch_shapes=[pltpu.VMEM(x.shape, x.dtype) for x in given]
        + scratch()
        + [
            pltpu.VMEM((TABLE, 128), F32),
            pltpu.SemaphoreType.DMA((PARTS,)),
            pltpu.SemaphoreType.DMA((len(given),)),
        ],
        compiler_params=PARAMS,
        name="start",
    )(cols, slots, me, in_hbm(sens), recv, *[in_hbm(x) for x in given])
    kept = pltpu.with_memory_space_constraint(kept, pltpu.VMEM)
    flipped = pltpu.with_memory_space_constraint(flipped, pltpu.VMEM)
    residual, out, pick = pl.pallas_call(
        right_side_kernel,
        out_shape=(cells_shape(), gather, jax.ShapeDtypeStruct((CELL_ROWS, GROUP_DEVS * SLOTS), BF16)),
        in_specs=[VM] * 2,
        out_specs=(VM,) * 3,
        compiler_params=PARAMS,
        name="right_side",
    )(exchange(out), bent)
    direction = residual
    update = residual
    d_all = jnp.zeros((8, 128), F32)
    norm = jnp.zeros((8, 128), F32)
    for step in range(CG_STEPS):
        first, last = step == 0, step == CG_STEPS - 1
        out, bent, direction, norm, *tables = pl.pallas_call(
            functools.partial(step_kernel, first),
            out_shape=(
                sent(EXTRA),
                cells_shape(),
                cells_shape(),
                jax.ShapeDtypeStruct((8, 128), F32),
            )
            + (() if last else (jax.ShapeDtypeStruct((TABLE, 128), F32),)),
            in_specs=[SM] * 3 + [VM] * 11,
            out_specs=(VM,) * (4 if last else 5),
            scratch_shapes=([pltpu.VMEM((TABLE, 128), F32)] if last else []) + scratch(),
            compiler_params=PARAMS,
            name="step",
        )(cols, slots, me, kept, flipped, rows, exchange(out), residual, direction, d_all, norm, data_weight, nb, small)
        results = pl.pallas_call(
            functools.partial(update_kernel, first, last),
            out_shape=(cells_shape(), cells_shape()) + (() if last else (gather,)),
            in_specs=[VM] * 7,
            out_specs=(VM,) * (2 if last else 3),
            compiler_params=PARAMS,
            name="update",
        )(exchange(out), pick, bent, direction, residual, update, norm)
        update, residual = results[:2]
        if not last:
            d_all = tables[0]
            out = results[2]
    return update.reshape(-1), residual.reshape(-1)


def solution(mesh):
    own = P(AXES)
    part = P(("ref",) + AXES)
    in_specs = (P(AXES, None, None), own, own, P(None, AXES), own, own, own, part, part)
    return jax.shard_map(
        per_device, mesh=mesh, in_specs=in_specs, out_specs=(part, part), check_vma=False
    )
```

```python
import functools

import jax
import jax.numpy as jnp
from jax import lax
from jax.experimental import pallas as pl
from jax.experimental.pallas import tpu as pltpu
from jax.sharding import PartitionSpec as P

CG_STEPS = 3
beta_reg = 0.5

AXES = ("lines", "cells")
BLOCKS = 512
CHUNK = 512
START_CHUNK = 256
PARTS = BLOCKS // START_CHUNK
BATCH = 16
GROUP_DEVS = 64
ROWS = 32
CELL_ROWS = 32
TABLE = GROUP_DEVS * CELL_ROWS
SLOTS = 16
EXTRA = 8
F32 = jnp.float32
BF16 = jnp.bfloat16


def total(x):
    return jnp.sum(jnp.sum(x, axis=0, keepdims=True), axis=1, keepdims=True)


def smooth_group(g, win, nb_ref, small, offset, out):
    first = pl.multiple_of(g * 8, 8)
    sub = lax.broadcasted_iota(jnp.int32, (8, 128), 0)
    acc = jnp.zeros((8, 128), F32)
    lanes = []
    deltas = []
    for k in range(6):
        index = nb_ref[k, pl.ds(first, 8), :] - offset + 1024
        lanes.append(index & 127)
        deltas.append((index >> 7) - first - sub)
    for delta in range(17):
        source = win[pl.ds(first + delta, 8), :]
        for k in range(6):
            picked = jnp.take_along_axis(source, lanes[k], axis=1, mode="promise_in_bounds")
            acc = acc + jnp.where(deltas[k] == delta, picked, 0.0)
    own = win[pl.ds(first + 8, 8), :]
    out[pl.ds(first, 8), :] = (small[pl.ds(first, 8), :] + 6.0) * own - acc


def forward_blocks(flipped, cols, tab, temp, products, beside, flip=None):
    size = CHUNK if flip is None else START_CHUNK
    pieces = CELL_ROWS // 8 * size // BLOCKS

    def chunk(g, _):
        first = pl.multiple_of(g * size, size)
        if flip is not None:
            sens, wait = flip
            wait(g)
        for piece in range(pieces):
            beside(g * pieces + piece)
        for h in range(size // BATCH):
            base = first + h * BATCH
            for q in range(BATCH):
                temp[pl.ds(base + q, 1), :] = tab[pl.ds(cols[base + q], 1), :]
            left = temp[pl.ds(base, BATCH), :].astype(BF16)
            if flip is not None:
                blocks = [sens[base + q].T for q in range(BATCH)]
                for q in range(BATCH):
                    flipped[base + q] = blocks[q]
            else:
                blocks = [flipped[base + q] for q in range(BATCH)]
            out = jnp.dot(left, jnp.concatenate(blocks, axis=1), preferred_element_type=F32)
            for q in range(BATCH):
                products[pl.ds(base + q, 1), :] = out[q : q + 1, q * 128 : (q + 1) * 128]
        return 0

    lax.fori_loop(0, BLOCKS // size, chunk, 0)


def row_hot(rows):
    return (lax.broadcasted_iota(jnp.int32, (ROWS, BLOCKS), 0) == rows[...]).astype(BF16)


def sum_rows(hot, products):
    value = products[...]
    high = value.astype(BF16)
    rest = value - high.astype(F32)
    middle = rest.astype(BF16)
    low = (rest - middle.astype(F32)).astype(BF16)
    return (
        jnp.dot(hot, high, preferred_element_type=F32)
        + jnp.dot(hot, middle, preferred_element_type=F32)
        + jnp.dot(hot, low, preferred_element_type=F32)
    )


def backward_blocks(hot, weighted, slots, sens, lhs, spread):
    lhs[...] = lax.dot_general(
        hot, weighted, (((0,), (0,)), ((), ())), preferred_element_type=F32
    ).astype(BF16)
    spread[...] = jnp.zeros_like(spread)

    def chunk(g, _):
        first = pl.multiple_of(g * CHUNK, CHUNK)
        for h in range(CHUNK // BATCH):
            base = first + h * BATCH
            right = jnp.concatenate([sens[base + q] for q in range(BATCH)], axis=1)
            out = jnp.dot(lhs[pl.ds(base, BATCH), :], right, preferred_element_type=F32)
            for q in range(BATCH):
                spread[pl.ds(slots[base + q], 1), :] = out[q : q + 1, q * 128 : (q + 1) * 128]
        return 0

    lax.fori_loop(0, BLOCKS // CHUNK, chunk, 0)


def scalar_tile(scalar):
    high = scalar.astype(BF16).astype(F32)
    middle = (scalar - high).astype(BF16).astype(F32)
    low = scalar - high - middle
    sub = lax.broadcasted_iota(jnp.int32, (EXTRA, 128), 0)
    lane = lax.broadcasted_iota(jnp.int32, (EXTRA, 128), 1)
    place = sub * 128 + lane
    return jnp.where(
        place == 0, high, jnp.where(place == 1, middle, jnp.where(place == 2, low, 0.0))
    )


def write_payload(out, spread, tail_of):
    def owners(g, _):
        for q in range(8):
            o = g * 8 + q
            base = pl.multiple_of(o * SLOTS, SLOTS)
            out[o] = jnp.concatenate([spread[pl.ds(base, SLOTS), :], tail_of(o)], axis=0).astype(BF16)
        return 0

    lax.fori_loop(0, GROUP_DEVS // 8, owners, 0)


def model_kernel(model_hbm, reference_hbm, diff_out, out, model, reference_model, half, sems):
    first = pltpu.make_async_copy(model_hbm, model, sems.at[0])
    second = pltpu.make_async_copy(reference_hbm, reference_model, sems.at[1])
    first.start()
    second.start()
    first.wait()
    second.wait()
    diff = model[...] - reference_model[...]
    diff_out[...] = diff
    payload = jnp.concatenate([model[...], diff[:8], diff[-8:]], axis=0).astype(BF16)
    for q in range(8):
        half[q] = payload
    sends = [
        pltpu.make_async_copy(half, out.at[pl.ds(8 * g, 8)], sems.at[2 + g]) for g in range(GROUP_DEVS // 8)
    ]
    for send in sends:
        send.start()
    for send in sends:
        send.wait()


def start_kernel(
    cols, slots, me, sens_hbm, recv, *refs,
):
    given, (out, bent_out, sens, flipped), held = refs[:7], refs[7:11], refs[11:18]
    temp, products, lhs, spread, win, tab, sems, held_sems = refs[18:]
    diff, small, nb, rows, observed, data_weight, slot_cells = held
    copies = [
        pltpu.make_async_copy(source, target, held_sems.at[i])
        for i, (source, target) in enumerate(zip(given, held))
    ]
    for copy in copies:
        copy.start()

    def part(g):
        span = pl.ds(pl.multiple_of(g * START_CHUNK, START_CHUNK), START_CHUNK)
        return pltpu.make_async_copy(sens_hbm.at[span], sens.at[span], sems.at[g])

    for g in range(PARTS):
        part(g).start()
    for copy in copies:
        copy.wait()

    def owners(g, _):
        for q in range(8):
            o = g * 8 + q
            base = pl.multiple_of(o * CELL_ROWS, CELL_ROWS)
            tab[pl.ds(base, CELL_ROWS), :] = recv[o, pl.ds(0, CELL_ROWS), :].astype(F32)
        return 0

    lax.fori_loop(0, GROUP_DEVS // 8, owners, 0)
    mine = me[0]
    before = jnp.maximum(mine - 1, 0)
    after = jnp.minimum(mine + 1, GROUP_DEVS - 1)
    win[pl.ds(0, 8), :] = recv[before, pl.ds(CELL_ROWS, 16), :].astype(F32)[8:16]
    win[pl.ds(8, CELL_ROWS), :] = diff[...]
    win[pl.ds(8 + CELL_ROWS, 8), :] = recv[after, pl.ds(CELL_ROWS, 16), :].astype(F32)[0:8]
    beside = functools.partial(
        smooth_group, win=win, nb_ref=nb, small=small, offset=mine * (CELL_ROWS * 128), out=bent_out
    )
    forward_blocks(flipped, cols, tab, temp, products, beside, (sens, lambda g: part(g).wait()))
    hot = row_hot(rows)
    weight = data_weight[...]
    misfit = weight * weight * (sum_rows(hot, products) - observed[...])
    backward_blocks(hot, misfit.astype(BF16), slots, sens, lhs, spread)
    write_payload(out, spread, lambda o: slot_cells[o])


def step_kernel(
    first_step,
    cols, slots, me, sens, flipped, rows, recv, residual, direction, d_all_in, norm_in, data_weight, nb, small,
    out, bent_out, d_out, norm_out, d_all_out, temp, products, lhs, spread, win,
):
    def squares(g, acc):
        for q in range(8):
            r = recv[g * 8 + q].astype(F32)
            acc = acc + r * r
        return acc

    acc = lax.fori_loop(0, GROUP_DEVS // 8, squares, jnp.zeros((CELL_ROWS, 128), F32))
    norm = total(acc)
    norm_out[...] = jnp.broadcast_to(norm, (8, 128))
    beta = None if first_step else norm / norm_in[0:1, 0:1]

    def owners(g, _):
        for q in range(8):
            o = g * 8 + q
            base = pl.multiple_of(o * CELL_ROWS, CELL_ROWS)
            d = recv[o].astype(F32)
            if not first_step:
                d = d + beta * d_all_in[pl.ds(base, CELL_ROWS), :]
            d_all_out[pl.ds(base, CELL_ROWS), :] = d
        return 0

    lax.fori_loop(0, GROUP_DEVS // 8, owners, 0)
    d_own = residual[...]
    if not first_step:
        d_own = d_own + beta * direction[...]
    d_out[...] = d_own
    mine = me[0]
    base = mine * CELL_ROWS
    before = pl.multiple_of(jnp.maximum(base - 8, 0), 8)
    after = pl.multiple_of(jnp.minimum(base + CELL_ROWS, TABLE - 8), 8)
    win[pl.ds(0, 8), :] = d_all_out[pl.ds(before, 8), :]
    win[pl.ds(8, CELL_ROWS), :] = d_own
    win[pl.ds(8 + CELL_ROWS, 8), :] = d_all_out[pl.ds(after, 8), :]
    beside = functools.partial(
        smooth_group, win=win, nb_ref=nb, small=small, offset=mine * (CELL_ROWS * 128), out=bent_out
    )
    forward_blocks(flipped, cols, d_all_out, temp, products, beside)
    hot = row_hot(rows)
    weight = data_weight[...]
    predicted = sum_rows(hot, products)
    weighted = (weight * weight * predicted).astype(BF16)
    curvature = total(predicted * weighted.astype(F32)) + beta_reg * total(d_own * bent_out[...])
    backward_blocks(hot, weighted, slots, sens, lhs, spread)
    tail = scalar_tile(curvature)
    write_payload(out, spread, lambda o: tail)


def gathered_sum(recv, pick):
    values = recv[:, 0:SLOTS, :].reshape(GROUP_DEVS * SLOTS, 128)
    return jnp.dot(pick, values, preferred_element_type=F32)


def broadcast_out(out, value):
    half = value.astype(BF16)

    def owners(g, _):
        for q in range(8):
            out[g * 8 + q] = half
        return 0

    lax.fori_loop(0, GROUP_DEVS // 8, owners, 0)


def right_side_kernel(recv, bent, r_out, out, pick_out, cells):
    def owners(g, _):
        for q in range(8):
            o = g * 8 + q
            cells[pl.ds(o, 1), :] = recv[o].astype(F32)[SLOTS : SLOTS + 1]
        return 0

    lax.fori_loop(0, GROUP_DEVS // 8, owners, 0)
    width = GROUP_DEVS * SLOTS
    spread = (
        lax.broadcasted_iota(jnp.int32, (128, width), 1) % SLOTS
        == lax.broadcasted_iota(jnp.int32, (128, width), 0)
    ).astype(BF16)
    everywhere = jnp.dot(cells[...].astype(BF16), spread, preferred_element_type=F32)
    mine = (
        lax.broadcasted_iota(jnp.int32, (GROUP_DEVS, width), 1) // SLOTS
        == lax.broadcasted_iota(jnp.int32, (GROUP_DEVS, width), 0)
    )
    cell = jnp.sum(jnp.where(mine, everywhere, 0.0), axis=0, keepdims=True).astype(jnp.int32)
    pick = (lax.broadcasted_iota(jnp.int32, (CELL_ROWS, width), 0) == cell).astype(BF16)
    pick_out[...] = pick
    r = -(gathered_sum(recv, pick) + beta_reg * bent[...])
    r_out[...] = r
    broadcast_out(out, r)


def update_kernel(first_step, last_step, recv, pick, bent, direction, residual, update, norm, u_out, r_out, *out):
    sums = gathered_sum(recv, pick[...])

    def tails(g, acc):
        for q in range(8):
            acc = acc + recv[g * 8 + q].astype(F32)[SLOTS:]
        return acc

    curvature = total(lax.fori_loop(0, GROUP_DEVS // 8, tails, jnp.zeros((EXTRA, 128), F32)))
    alpha = norm[0:1, 0:1] / curvature
    d = direction[...]
    u_out[...] = alpha * d if first_step else update[...] + alpha * d
    r = residual[...] - alpha * (sums + beta_reg * bent[...])
    r_out[...] = r
    if not last_step:
        broadcast_out(out[0], r)


VM = pl.BlockSpec(memory_space=pltpu.VMEM)
SM = pl.BlockSpec(memory_space=pltpu.SMEM)
HB = pl.BlockSpec(memory_space=pltpu.HBM)
PARAMS = pltpu.CompilerParams(vmem_limit_bytes=12 << 20)


def in_hbm(x):
    return pltpu.with_memory_space_constraint(x, pltpu.HBM)


def cells_shape():
    return jax.ShapeDtypeStruct((CELL_ROWS, 128), F32)


def scratch():
    return [
        pltpu.VMEM((BLOCKS, 128), F32),
        pltpu.VMEM((BLOCKS, 128), F32),
        pltpu.VMEM((BLOCKS, 128), BF16),
        pltpu.VMEM((GROUP_DEVS * SLOTS, 128), F32),
        pltpu.VMEM((CELL_ROWS + 16, 128), F32),
    ]


def slot_lists(block_cols):
    ids = jnp.arange(BLOCKS, dtype=jnp.int32)
    owners = block_cols // CELL_ROWS
    shared = (owners[None, :] == owners[:, None]) & (ids[None, :] < ids[:, None])
    slots = owners * SLOTS + jnp.sum(shared.astype(jnp.int32), axis=1)
    taken = slots[None, :] == jnp.arange(GROUP_DEVS * SLOTS, dtype=jnp.int32)[:, None]
    cell = jnp.sum(jnp.where(taken, (block_cols % CELL_ROWS)[None, :] + 1, 0), axis=1) - 1
    cell = jnp.maximum(cell, 0).astype(F32).reshape(GROUP_DEVS, 1, SLOTS)
    return slots, jnp.pad(cell, ((0, 0), (0, EXTRA - 1), (0, 128 - SLOTS)))


def per_device(
    sens, block_rows, block_cols, neighbours, observed, data_weight, smallness, model, reference_model
):
    cols = block_cols
    slots, slot_cells = slot_lists(block_cols)
    rows = block_rows.reshape(1, BLOCKS)
    me = lax.axis_index(AXES).astype(jnp.int32).reshape(1)
    nb = neighbours.reshape(6, CELL_ROWS, 128)
    observed = observed.reshape(ROWS, 128)
    data_weight = data_weight.reshape(ROWS, 128)
    small = smallness.reshape(CELL_ROWS, 128)
    model = model.reshape(CELL_ROWS, 128)

    def exchange(x):
        return lax.all_to_all(x, AXES, 0, 0, tiled=True)

    diff, out = pl.pallas_call(
        model_kernel,
        out_shape=(cells_shape(), pltpu.HBM((GROUP_DEVS, CELL_ROWS + 16, 128), BF16)),
        in_specs=[HB] * 2,
        out_specs=(VM, HB),
        scratch_shapes=[pltpu.VMEM((CELL_ROWS, 128), F32)] * 2
        + [pltpu.VMEM((8, CELL_ROWS + 16, 128), BF16), pltpu.SemaphoreType.DMA((2 + GROUP_DEVS // 8,))],
        compiler_params=PARAMS,
        name="model",
    )(in_hbm(model), in_hbm(reference_model.reshape(CELL_ROWS, 128)))
    recv = exchange(out)
    def sent(rows):
        return jax.ShapeDtypeStruct((GROUP_DEVS, SLOTS + rows, 128), BF16)

    gather = jax.ShapeDtypeStruct((GROUP_DEVS, CELL_ROWS, 128), BF16)
    given = (diff, small, nb, rows, observed, data_weight, slot_cells)
    out, bent, kept, flipped = pl.pallas_call(
        start_kernel,
        out_shape=(sent(EXTRA), cells_shape(), pltpu.VMEM(sens.shape, BF16), pltpu.VMEM(sens.shape, BF16)),
        in_specs=[SM] * 3 + [HB, VM] + [HB] * 7,
        out_specs=(VM,) * 4,
        scratch_shapes=[pltpu.VMEM(x.shape, x.dtype) for x in given]
        + scratch()
        + [
            pltpu.VMEM((TABLE, 128), F32),
            pltpu.SemaphoreType.DMA((PARTS,)),
            pltpu.SemaphoreType.DMA((len(given),)),
        ],
        compiler_params=PARAMS,
        name="start",
    )(cols, slots, me, in_hbm(sens), recv, *[in_hbm(x) for x in given])
    kept = pltpu.with_memory_space_constraint(kept, pltpu.VMEM)
    flipped = pltpu.with_memory_space_constraint(flipped, pltpu.VMEM)
    residual, out, pick = pl.pallas_call(
        right_side_kernel,
        out_shape=(cells_shape(), gather, jax.ShapeDtypeStruct((CELL_ROWS, GROUP_DEVS * SLOTS), BF16)),
        in_specs=[VM] * 2,
        out_specs=(VM,) * 3,
        scratch_shapes=[pltpu.VMEM((GROUP_DEVS, 128), F32)],
        compiler_params=PARAMS,
        name="right_side",
    )(exchange(out), bent)
    direction = residual
    update = residual
    d_all = jnp.zeros((8, 128), F32)
    norm = jnp.zeros((8, 128), F32)
    for step in range(CG_STEPS):
        first, last = step == 0, step == CG_STEPS - 1
        out, bent, direction, norm, *tables = pl.pallas_call(
            functools.partial(step_kernel, first),
            out_shape=(
                sent(EXTRA),
                cells_shape(),
                cells_shape(),
                jax.ShapeDtypeStruct((8, 128), F32),
            )
            + (() if last else (jax.ShapeDtypeStruct((TABLE, 128), F32),)),
            in_specs=[SM] * 3 + [VM] * 11,
            out_specs=(VM,) * (4 if last else 5),
            scratch_shapes=([pltpu.VMEM((TABLE, 128), F32)] if last else []) + scratch(),
            compiler_params=PARAMS,
            name="step",
        )(cols, slots, me, kept, flipped, rows, exchange(out), residual, direction, d_all, norm, data_weight, nb, small)
        results = pl.pallas_call(
            functools.partial(update_kernel, first, last),
            out_shape=(cells_shape(), cells_shape()) + (() if last else (gather,)),
            in_specs=[VM] * 7,
            out_specs=(VM,) * (2 if last else 3),
            compiler_params=PARAMS,
            name="update",
        )(exchange(out), pick, bent, direction, residual, update, norm)
        update, residual = results[:2]
        if not last:
            d_all = tables[0]
            out = results[2]
    return update.reshape(-1), residual.reshape(-1)


def solution(mesh):
    own = P(AXES)
    part = P(("ref",) + AXES)
    in_specs = (P(AXES, None, None), own, own, P(None, AXES), own, own, own, part, part)
    return jax.shard_map(
        per_device, mesh=mesh, in_specs=in_specs, out_specs=(part, part), check_vma=False
    )
```
